256 devices in a mesh: grp: 16 (over y, x), sq: 16 (over z, core).
Axes of the slice: x: 4, y: 4, z: 8, core: 2. Of those that a mesh axis runs over, the one named last changes fastest.
Arguments:
- queries: bfloat16 [65536, 4096], P(('grp', 'sq')), parts along dimension 0, may hold values from -6 to 6
- keys: bfloat16 [65536, 1024], P(('grp', 'sq')), parts along dimension 0, may hold values from -6 to 6
- values: bfloat16 [65536, 1024], P(('grp', 'sq')), parts along dimension 0, may hold values from -6 to 6
- tile_lists: int32 [512, 32, 16], P('grp'), parts along dimension 0, may hold values from 0 to 31, as said below
- tile_counts: int32 [512, 32], P('grp'), parts along dimension 0, may hold values from 1 to 16, as said below
Outputs:
- attended: bfloat16 [65536, 4096], P(('grp', 'sq')), parts along dimension 0
The draws below stay inside these ranges and needn't reach their ends.
There are 16 independent parts, one for each index of `grp`. The reference program is written for one: setup_inputs(seed, part) draws one part's arguments, and reference() takes and returns one part's arrays. A program takes and returns all parts, laid end to end along the dimension named above; each array names one. Nothing has to cross between parts.
Inputs may be any that keep to these rules, and one draw needn't show every extreme that they name: tile_counts[h, b] = min(b + 1, c_h) with a cap c_h for each head h; at least one head has cap 16. tile_lists[h, b, j] for j < tile_counts[h, b] are distinct key blocks from 0 to b, the first one being b; the later entries equal b.
All inputs are finite; a program needn't handle non-finite values.
Results may differ from the reference program's by a relative error of at most 0.0042.
Values may be sent and summed in bfloat16 or wider, within the bound.
A program may use at most 64 MiB of HBM per device.

```python
import jax
import jax.numpy as jnp
from jax import lax

HEADS = 32
KV_HEADS = 8
HEAD_DIM = 128
TILE = 128
MAX_TILES = 16
SEQ = 4096
BLOCKS = 32


def draw_queries(key, part):
    key = jax.random.fold_in(key, 1)
    result = jnp.clip(jax.random.normal(key, (SEQ, HEADS * HEAD_DIM), jnp.float32), -4.5, 4.5)
    return result.astype(jnp.bfloat16)


def draw_keys(key, part):
    key = jax.random.fold_in(key, 2)
    result = jnp.clip(jax.random.normal(key, (SEQ, KV_HEADS * HEAD_DIM), jnp.float32), -4.5, 4.5)
    return result.astype(jnp.bfloat16)


def sparse_plan(key):
    shuffle = jax.random.permutation(jax.random.fold_in(key, 201), HEADS)
    light_cap = jax.random.randint(jax.random.fold_in(key, 202), (HEADS,), 2, max(3, MAX_TILES // 2))
    head_cap = jnp.where(shuffle < 4, MAX_TILES, light_cap).astype(jnp.int32)
    block_ids = jnp.arange(BLOCKS, dtype=jnp.int32)
    counts = jnp.minimum(block_ids[None, :] + 1, head_cap[:, None]).astype(jnp.int32)
    vertical = jax.random.randint(jax.random.fold_in(key, 203), (HEADS, BLOCKS), 0, 1000)
    diagonal_score = jax.random.randint(jax.random.fold_in(key, 204), (HEADS, BLOCKS), 0, 1000)
    offsets = jnp.clip(block_ids[:, None] - block_ids[None, :], 0, BLOCKS - 1)
    slash_at = jnp.take(diagonal_score, offsets, axis=1)
    priority = jnp.maximum(vertical[:, None, :], slash_at) * BLOCKS + block_ids[None, None, :]
    is_diag = (block_ids[:, None] == block_ids[None, :])[None, :, :]
    is_later = (block_ids[None, :] > block_ids[:, None])[None, :, :]
    priority = jnp.where(is_diag, 1001 * BLOCKS, jnp.where(is_later, -1, priority)).astype(jnp.int32)
    picks = lax.top_k(priority, MAX_TILES)[1].astype(jnp.int32)
    used = jnp.arange(MAX_TILES, dtype=jnp.int32)[None, None, :] < counts[:, :, None]
    tile_picks = jnp.where(used, picks, block_ids[None, :, None]).astype(jnp.int32)
    return (tile_picks, counts)


def draw_tile_lists(key, part):
    tile_picks, counts = sparse_plan(key)
    return tile_picks


def draw_tile_counts(key, part):
    tile_picks, counts = sparse_plan(key)
    return counts


def block_levels(rng, shape, pieces, low, largest):
    gain, own = 1.0, jax.random.fold_in(rng, 6)
    for dim, shards_of in pieces:
        steps = jnp.exp(jax.random.uniform(jax.random.fold_in(own, dim), (shards_of,), jnp.float32, low / len(pieces), largest / len(pieces)))
        gain = gain * jnp.repeat(steps, shape[dim] // shards_of).reshape([-1 if axis == dim else 1 for axis in range(len(shape))])
    return gain


def gaussian(rng, shape, scale, limit, split=(), held_as=jnp.bfloat16):
    factor_of = block_levels(rng, shape, split, -0.22, 0.18) if split else 1.0
    values = jax.random.normal(rng, shape, jnp.float32) * scale * factor_of
    return jnp.minimum(jnp.maximum(values, -limit), limit).astype(held_as)


def setup_inputs(seed: int = 0, part: int = 0) -> dict:
    key_of = jax.random.split(jax.random.key(seed), 6)
    own_keys = jax.random.split(jax.random.fold_in(key_of[5], part), 6)
    queries = draw_queries(jax.random.fold_in(jax.random.fold_in(key_of[5], part), 71), part)
    keys = draw_keys(jax.random.fold_in(jax.random.fold_in(key_of[5], part), 71), part)
    values = gaussian(own_keys[2], (SEQ, KV_HEADS * HEAD_DIM), 1.0, 6.0, ((0, 16),))
    tile_lists = draw_tile_lists(jax.random.fold_in(jax.random.fold_in(key_of[5], part), 71), part)
    tile_counts = draw_tile_counts(jax.random.fold_in(jax.random.fold_in(key_of[5], part), 71), part)
    return {"queries": queries, "keys": keys, "values": values, "tile_lists": tile_lists, "tile_counts": tile_counts}


def attend_head(query_head, key_head, value_head, lists, counts):
    length, width = query_head.shape
    blocks = length // TILE
    query_tiles = query_head.astype(jnp.float32).reshape(blocks, TILE, width)
    key_tiles = key_head.astype(jnp.float32).reshape(blocks, TILE, width)
    value_tiles = value_head.astype(jnp.float32).reshape(blocks, TILE, width)
    scaling = width ** -0.5
    offsets = jnp.arange(TILE, dtype=jnp.int32)
    query_position = jnp.arange(blocks, dtype=jnp.int32)[:, None] * TILE + offsets[None, :]

    def advance(tile_turn, state_now):
        run_max, run_sum, running = state_now
        chosen = lax.dynamic_index_in_dim(lists, tile_turn, axis=1, keepdims=False)
        is_live = tile_turn < counts
        key_block = jnp.take(key_tiles, chosen, axis=0)
        value_block = jnp.take(value_tiles, chosen, axis=0)
        scores = jnp.einsum("bid,bjd->bij", query_tiles, key_block) * scaling
        key_position = chosen[:, None] * TILE + offsets[None, :]
        allowed = (key_position[:, None, :] <= query_position[:, :, None]) & is_live[:, None, None]
        masked = jnp.where(allowed, scores, jnp.float32(-1e30))
        new_max = jnp.maximum(run_max, jnp.max(masked, axis=2))
        weights = jnp.where(allowed, jnp.exp(masked - new_max[:, :, None]), jnp.float32(0.0))
        factor = jnp.exp(run_max - new_max)
        run_sum = run_sum * factor + jnp.sum(weights, axis=2)
        rounded = weights.astype(jnp.bfloat16).astype(jnp.float32)
        running = running * factor[:, :, None] + jnp.einsum("bij,bjd->bid", rounded, value_block)
        return new_max, run_sum, running

    initial = (jnp.full((blocks, TILE), -1e30, jnp.float32), jnp.zeros((blocks, TILE), jnp.float32), jnp.zeros((blocks, TILE, width), jnp.float32))
    run_max, run_sum, running = lax.fori_loop(jnp.int32(0), jnp.max(counts).astype(jnp.int32), advance, initial)
    return (running / run_sum[:, :, None]).astype(jnp.bfloat16).reshape(length, width)


def reference(queries, keys, values, tile_lists, tile_counts):
    group_size = HEADS // KV_HEADS
    query_heads = queries.reshape(SEQ, HEADS, HEAD_DIM)
    key_heads = keys.reshape(SEQ, KV_HEADS, HEAD_DIM)
    value_heads = values.reshape(SEQ, KV_HEADS, HEAD_DIM)

    def one_head(head_id):
        shared = head_id // group_size
        return attend_head(query_heads[:, head_id], key_heads[:, shared], value_heads[:, shared], tile_lists[head_id], tile_counts[head_id])

    results = lax.map(one_head, jnp.arange(HEADS, dtype=jnp.int32))
    return jnp.transpose(results, (1, 0, 2)).reshape(SEQ, HEADS * HEAD_DIM)
```

```python
import functools

import jax
import jax.numpy as jnp
from jax import lax
from jax.experimental import pallas as pl
from jax.experimental.pallas import tpu as pltpu
from jax.sharding import PartitionSpec as P

MESH = pl.DeviceIdType.MESH
HEAD_DIM = 128
TILE = 128
CHIPS = 8
LAG = 2
LOW = -1e30
LOG2E = 1.4426950408889634

DO_COMM = True
DO_COMPUTE = True


def kernel(kv_count, group, tiles, q_ref, k_ref, v_ref, lists_ref, counts_ref, out_ref, *scratch):
    kv = scratch[:kv_count]
    q_t, scores, recv, plus_sem, minus_sem, twin_sem = scratch[kv_count:]
    rank = lax.axis_index("sq")
    z, core = rank // 2, rank % 2
    right = lax.rem(z + 1, CHIPS) * 2 + core
    left = lax.rem(z + CHIPS - 1, CHIPS) * 2 + core
    twin = z * 2 + (1 - core)

    barrier = pltpu.get_barrier_semaphore()
    for other in (left, right, twin):
        pl.semaphore_signal(barrier, inc=1, device_id={"sq": other}, device_id_type=MESH)

    for h in range(kv_count):
        cols = pl.ds(h * HEAD_DIM, HEAD_DIM)
        for half in range(2):
            rows = pl.ds(half * TILE, TILE)
            kv[h][rank * 2 + half, 0] = k_ref[rows, cols]
            kv[h][rank * 2 + half, 1] = v_ref[rows, cols].T
    pl.semaphore_wait(barrier, 3)

    def piece(h, source, sem, target):
        at = kv[h].at[pl.ds(source * 2, 2)]
        return pltpu.make_async_remote_copy(
            src_ref=at,
            dst_ref=at,
            send_sem=sem,
            recv_sem=recv.at[h, source],
            device_id={"sq": target},
            device_id_type=MESH,
        )

    def goes_up(h, j):
        source = z - j
        near = (source >= 0) & (z < CHIPS - 1)
        if j < 3:
            return near, source
        return near & (source == 3) & (h % 2 == 0), source

    def goes_down(h, j):
        source = lax.rem(z + j, CHIPS)
        return source <= (2 if h % 2 == 0 else 3), source

    def from_below(h, j):
        source = z - j
        if j < 4:
            return source >= 0, source
        return (source == 3) & (h % 2 == 0), source

    def from_above(h, j):
        source = lax.rem(z + j, CHIPS)
        return source <= (2 if h % 2 == 0 else 3), source

    def up(h, j, source):
        return piece(h, source * 2 + core, plus_sem.at[h, j], right)

    def down(h, j, source):
        return piece(h, source * 2 + core, minus_sem.at[h, j], left)

    def across(h, source):
        return piece(h, source * 2 + core, twin_sem.at[h, source], twin)

    def own(h):
        for go, make in ((goes_up, up), (goes_down, down)):
            cond, source = go(h, 0)

            @pl.when(cond)
            def _():
                make(h, 0, source).start()

        across(h, z).start()

    def arrive(h, j):
        for come, go, make in ((from_below, goes_up, up), (from_above, goes_down, down)):
            cond, source = come(h, j)

            @pl.when(cond)
            def _():
                piece(h, source * 2 + core, plus_sem.at[h, 0], right).wait_recv()
                if j < 4:
                    more, _ = go(h, j)

                    @pl.when(more)
                    def _():
                        make(h, j, source).start()

                @pl.when(source < z)
                def _():
                    across(h, source).start()

    def settle(h):
        def one(source, carry):
            piece(h, source * 2 + 1 - core, plus_sem.at[h, 0], right).wait_recv()
            return carry

        lax.fori_loop(0, z + 1, one, 0)

    def sent(h):
        for j in range(4):
            for go, make in ((goes_up, up), (goes_down, down)):
                cond, source = go(h, j)

                @pl.when(cond)
                def _():
                    make(h, j, source).wait_send()

        def one(source, carry):
            across(h, source).wait_send()
            return carry

        lax.fori_loop(0, z + 1, one, 0)

    key_at = lax.broadcasted_iota(jnp.int32, (TILE, TILE), 0)
    query_at = lax.broadcasted_iota(jnp.int32, (TILE, TILE), 1)
    causal = key_at <= query_at
    factor = (HEAD_DIM ** -0.5) * LOG2E

    def attend(h, unit):
        head = h * group + unit // 2
        half = unit % 2
        block = rank * 2 + half
        count = counts_ref[head, block]
        turned = q_t[head * 2 + half]
        best = jnp.full((8, TILE), LOW, jnp.float32)
        for j in range(tiles):
            at = lists_ref[head, block, j]
            s = jnp.dot(kv[h][at, 0], turned, preferred_element_type=jnp.float32)
            if j == 0:
                s = jnp.where(causal, s, LOW)
            scores[j] = s
            top = jnp.max(s.reshape(TILE // 8, 8, TILE), axis=0)
            best = jnp.maximum(best, jnp.where(j < count, top, LOW))
        best = jnp.max(best, axis=0, keepdims=True) * factor
        total = jnp.zeros((8, TILE), jnp.float32)
        result = jnp.zeros((HEAD_DIM, TILE), jnp.float32)
        for j in range(tiles):
            at = lists_ref[head, block, j]
            floor = jnp.where(j < count, best, 1e30)
            weights = jnp.exp2(scores[j] * factor - floor)
            total = total + jnp.sum(weights.reshape(TILE // 8, 8, TILE), axis=0)
            result = result + jnp.dot(
                kv[h][at, 1], weights.astype(jnp.bfloat16), preferred_element_type=jnp.float32
            )
        total = jnp.sum(total, axis=0, keepdims=True)
        done = (result * (1.0 / total)).T.astype(jnp.bfloat16)
        out_ref[
            pl.ds(pl.multiple_of(half * TILE, TILE), TILE),
            pl.ds(pl.multiple_of(head * HEAD_DIM, HEAD_DIM), HEAD_DIM),
        ] = done

    def turn(head, carry):
        for half in range(2):
            cols = pl.ds(pl.multiple_of(head * HEAD_DIM, HEAD_DIM), HEAD_DIM)
            q_t[head * 2 + half] = q_ref[pl.ds(half * TILE, TILE), cols].T
        return carry

    last = kv_count - 1 + 4 * LAG
    for t in range(last + 1):
        if DO_COMM:
            if t < kv_count:
                own(t)
            for j in range(1, 5):
                h = t - LAG * j
                if 0 <= h < kv_count:
                    arrive(h, j)
        if t == 0:
            lax.fori_loop(0, kv_count * group, turn, 0)
        h = t - 4 * LAG
        if 0 <= h < kv_count:
            if DO_COMM:
                settle(h)
            if DO_COMPUTE:

                def step(unit, carry):
                    attend(h, unit)
                    return carry

                lax.fori_loop(0, group * 2, step, 0)
    if DO_COMM:
        for h in range(kv_count):
            sent(h)


def body(queries, keys, values, tile_lists, tile_counts):
    rows, width = queries.shape
    kv_count = keys.shape[1] // HEAD_DIM
    heads, blocks, tiles = tile_lists.shape
    group = heads // kv_count
    ranks = lax.axis_size("sq")
    vmem = pl.BlockSpec(memory_space=pltpu.VMEM)
    smem = pl.BlockSpec(memory_space=pltpu.SMEM)
    return pl.pallas_call(
        functools.partial(kernel, kv_count, group, tiles),
        out_shape=jax.ShapeDtypeStruct((rows, width), jnp.bfloat16),
        in_specs=[vmem, vmem, vmem, smem, smem],
        out_specs=vmem,
        scratch_shapes=[pltpu.VMEM((blocks, 2, TILE, HEAD_DIM), jnp.bfloat16)] * kv_count
        + [
            pltpu.VMEM((heads * 2, HEAD_DIM, TILE), jnp.bfloat16),
            pltpu.VMEM((tiles, TILE, TILE), jnp.float32),
            pltpu.SemaphoreType.DMA((kv_count, ranks)),
            pltpu.SemaphoreType.DMA((kv_count, 4)),
            pltpu.SemaphoreType.DMA((kv_count, 4)),
            pltpu.SemaphoreType.DMA((kv_count, ranks // 2)),
        ],
        compiler_params=pltpu.CompilerParams(
            collective_id=0, has_side_effects=True, vmem_limit_bytes=48 * 1024 * 1024
        ),
    )(queries, keys, values, tile_lists, tile_counts)


def solution(mesh):
    placed = (
        P(("grp", "sq"), None),
        P(("grp", "sq"), None),
        P(("grp", "sq"), None),
        P("grp", None, None),
        P("grp", None),
    )
    return jax.shard_map(
        body, mesh=mesh, in_specs=placed, out_specs=P(("grp", "sq"), None), check_vma=False
    )
```

```python
import functools

import jax
import jax.numpy as jnp
from jax import lax
from jax.experimental import pallas as pl
from jax.experimental.pallas import tpu as pltpu
from jax.sharding import PartitionSpec as P

MESH = pl.DeviceIdType.MESH
HEAD_DIM = 128
TILE = 128
CHIPS = 8
LAG = 1
JOINT = 4
LOW = -1e30
LOG2E = 1.4426950408889634

DO_COMM = True
DO_COMPUTE = True


def kernel(kv_count, group, tiles, q_hbm, k_hbm, v_hbm, lists_hbm, counts_hbm, out_ref, *scratch):
    kv = scratch[:kv_count]
    q_ref, k_ref, v_ref, lists_ref, counts_ref, q_t = scratch[kv_count : kv_count + 6]
    wide_a, wide_b, scores_a, scores_b, best_a, best_b = scratch[kv_count + 6 : kv_count + 12]
    load, recv, plus_sem, minus_sem, twin_sem = scratch[kv_count + 12 :]
    loads = [
        pltpu.make_async_copy(src, dst, load.at[i])
        for i, (src, dst) in enumerate(
            (
                (k_hbm, k_ref),
                (v_hbm, v_ref),
                (q_hbm, q_ref),
                (lists_hbm, lists_ref),
                (counts_hbm, counts_ref),
            )
        )
    ]
    for copy in loads:
        copy.start()
    rank = lax.axis_index("sq")
    z, core = rank // 2, rank % 2
    right = lax.rem(z + 1, CHIPS) * 2 + core
    left = lax.rem(z + CHIPS - 1, CHIPS) * 2 + core
    twin = z * 2 + (1 - core)

    barrier = pltpu.get_barrier_semaphore()
    for other in (left, right, twin):
        pl.semaphore_signal(barrier, inc=1, device_id={"sq": other}, device_id_type=MESH)

    wide_a[...] = jnp.zeros_like(wide_a)
    wide_b[...] = jnp.zeros_like(wide_b)
    loads[0].wait()
    loads[1].wait()
    for h in range(kv_count):
        cols = pl.ds(h * HEAD_DIM, HEAD_DIM)
        for half in range(2):
            rows = pl.ds(half * TILE, TILE)
            kv[h][rank * 2 + half, 0] = k_ref[rows, cols]
            kv[h][rank * 2 + half, 1] = v_ref[rows, cols].T
    pl.semaphore_wait(barrier, 3)

    def piece(h, source, sem, target):
        at = kv[h].at[pl.ds(source * 2, 2)]
        return pltpu.make_async_remote_copy(
            src_ref=at,
            dst_ref=at,
            send_sem=sem,
            recv_sem=recv.at[h, source],
            device_id={"sq": target},
            device_id_type=MESH,
        )

    def goes_up(h, j):
        source = z - j
        near = (source >= 0) & (z < CHIPS - 1)
        if j < 3:
            return near, source
        return near & (source == 3) & (h % 2 == 0), source

    def goes_down(h, j):
        source = lax.rem(z + j, CHIPS)
        return source <= (2 if h % 2 == 0 else 3), source

    def from_below(h, j):
        source = z - j
        if j < 4:
            return source >= 0, source
        return (source == 3) & (h % 2 == 0), source

    def from_above(h, j):
        source = lax.rem(z + j, CHIPS)
        return source <= (2 if h % 2 == 0 else 3), source

    def up(h, j, source):
        return piece(h, source * 2 + core, plus_sem.at[h, j], right)

    def down(h, j, source):
        return piece(h, source * 2 + core, minus_sem.at[h, j], left)

    def across(h, source):
        return piece(h, source * 2 + core, twin_sem.at[h, source], twin)

    def own(h):
        for go, make in ((goes_up, up), (goes_down, down)):
            cond, source = go(h, 0)

            @pl.when(cond)
            def _():
                make(h, 0, source).start()

        across(h, z).start()

    def arrive(h, j):
        for come, go, make in ((from_below, goes_up, up), (from_above, goes_down, down)):
            cond, source = come(h, j)

            @pl.when(cond)
            def _():
                piece(h, source * 2 + core, plus_sem.at[h, 0], right).wait_recv()
                if j < 4:
                    more, _ = go(h, j)

                    @pl.when(more)
                    def _():
                        make(h, j, source).start()

                @pl.when(source < z)
                def _():
                    across(h, source).start()

    def settle(h):
        def one(source, carry):
            piece(h, source * 2 + 1 - core, plus_sem.at[h, 0], right).wait_recv()
            return carry

        lax.fori_loop(0, z + 1, one, 0)

    def sent(h):
        for j in range(4):
            for go, make in ((goes_up, up), (goes_down, down)):
                cond, source = go(h, j)

                @pl.when(cond)
                def _():
                    make(h, j, source).wait_send()

        def one(source, carry):
            across(h, source).wait_send()
            return carry

        lax.fori_loop(0, z + 1, one, 0)

    key_at = lax.broadcasted_iota(jnp.int32, (TILE, 2 * TILE), 0)
    query_at = lax.rem(lax.broadcasted_iota(jnp.int32, (TILE, 2 * TILE), 1), TILE)
    causal = key_at <= query_at
    factor = (HEAD_DIM**-0.5) * LOG2E

    def pair(first, second):
        return jnp.concatenate([first, second], axis=1)

    def side(x, half):
        return x[:, half * TILE : (half + 1) * TILE]

    def listed(head, half, j):
        return lists_ref[head, j, rank * 2 + half]

    def live(head, j, x, other):
        return pair(
            *[
                jnp.where(j < counts_ref[head, rank * 2 + half], side(x, half), other)
                for half in range(2)
            ]
        )

    def score(h, head, wide, scores, best_ref):
        for half in range(2):
            at = pl.ds(half * TILE, TILE)
            wide[at, at] = q_t[head * 2 + half]
        listed_keys = [
            pair(*[kv[h][listed(head, half, j), 0] for half in range(2)]) for j in range(tiles)
        ]
        all_scores = jnp.dot(
            jnp.concatenate(listed_keys, axis=0), wide[...], preferred_element_type=jnp.float32
        )
        best = jnp.full((8, 2 * TILE), LOW, jnp.float32)
        for j in range(tiles):
            s = all_scores[j * TILE : (j + 1) * TILE]
            if j == 0:
                s = jnp.where(causal, s, LOW)
            scores[j] = s
            top = jnp.max(s.reshape(TILE // 8, 8, 2 * TILE), axis=0)
            best = jnp.maximum(best, live(head, j, top, LOW))
        best_ref[...] = best

    def attend(h, head, scores, best_ref):
        best = jnp.max(best_ref[...], axis=0, keepdims=True) * factor
        total = jnp.zeros((8, 2 * TILE), jnp.float32)
        result = [jnp.zeros((HEAD_DIM, TILE), jnp.float32)] * 2
        for first in range(0, tiles, JOINT):
            weights = []
            for j in range(first, first + JOINT):
                w = jnp.exp2(scores[j] * factor - live(head, j, best, 1e30))
                total = total + jnp.sum(w.reshape(TILE // 8, 8, 2 * TILE), axis=0)
                weights.append(w.astype(jnp.bfloat16))
            weights = jnp.concatenate(weights, axis=0)
            for half in range(2):
                turned = [kv[h][listed(head, half, j), 1] for j in range(first, first + JOINT)]
                result[half] = result[half] + jnp.dot(
                    jnp.concatenate(turned, axis=1),
                    side(weights, half),
                    preferred_element_type=jnp.float32,
                )
        scale = 1.0 / jnp.sum(total, axis=0, keepdims=True)
        for half in range(2):
            out_ref[
                pl.ds(half * TILE, TILE),
                pl.ds(pl.multiple_of(head * HEAD_DIM, HEAD_DIM), HEAD_DIM),
            ] = (result[half] * side(scale, half)).T.astype(jnp.bfloat16)

    def attend_group(h):
        first = h * group
        score(h, first, wide_a, scores_a, best_a)

        def step(i, carry):
            head = first + 2 * i
            score(h, head + 1, wide_b, scores_b, best_b)
            attend(h, head, scores_a, best_a)
            score(h, jnp.minimum(head + 2, first + group - 1), wide_a, scores_a, best_a)
            attend(h, head + 1, scores_b, best_b)
            return carry

        lax.fori_loop(0, group // 2, step, 0)

    def turn(head, carry):
        for half in range(2):
            cols = pl.ds(pl.multiple_of(head * HEAD_DIM, HEAD_DIM), HEAD_DIM)
            q_t[head * 2 + half] = q_ref[pl.ds(half * TILE, TILE), cols].T
        return carry

    last = kv_count - 1 + 4 * LAG
    for t in range(last + 1):
        if DO_COMM:
            if t < kv_count:
                own(t)
            for j in range(1, 5):
                h = t - LAG * j
                if 0 <= h < kv_count:
                    arrive(h, j)
        if t == 0:
            for copy in loads[2:]:
                copy.wait()
            lax.fori_loop(0, kv_count * group, turn, 0)
        h = t - 4 * LAG
        if 0 <= h < kv_count:
            if DO_COMM:
                settle(h)
            if DO_COMPUTE:
                attend_group(h)
    if DO_COMM:
        for h in range(kv_count):
            sent(h)


def body(queries, keys, values, tile_lists, tile_counts):
    rows, width = queries.shape
    kv_count = keys.shape[1] // HEAD_DIM
    heads, blocks, tiles = tile_lists.shape
    group = heads // kv_count
    ranks = lax.axis_size("sq")
    any_place = pl.BlockSpec(memory_space=pl.ANY)
    scores = pltpu.VMEM((tiles, TILE, 2 * TILE), jnp.float32)
    wide = pltpu.VMEM((2 * TILE, 2 * TILE), jnp.bfloat16)
    best = pltpu.VMEM((8, 2 * TILE), jnp.float32)
    return pl.pallas_call(
        functools.partial(kernel, kv_count, group, tiles),
        out_shape=jax.ShapeDtypeStruct((rows, width), jnp.bfloat16),
        in_specs=[any_place] * 5,
        out_specs=pl.BlockSpec(memory_space=pltpu.VMEM),
        scratch_shapes=[pltpu.VMEM((blocks, 2, TILE, HEAD_DIM), jnp.bfloat16)] * kv_count
        + [
            pltpu.VMEM(queries.shape, jnp.bfloat16),
            pltpu.VMEM(keys.shape, jnp.bfloat16),
            pltpu.VMEM(values.shape, jnp.bfloat16),
            pltpu.SMEM((heads, tiles, blocks), jnp.int32),
            pltpu.SMEM(tile_counts.shape, jnp.int32),
            pltpu.VMEM((heads * 2, HEAD_DIM, TILE), jnp.bfloat16),
            wide,
            wide,
            scores,
            scores,
            best,
            best,
            pltpu.SemaphoreType.DMA((5,)),
            pltpu.SemaphoreType.DMA((kv_count, ranks)),
            pltpu.SemaphoreType.DMA((kv_count, 4)),
            pltpu.SemaphoreType.DMA((kv_count, 4)),
            pltpu.SemaphoreType.DMA((kv_count, ranks // 2)),
        ],
        compiler_params=pltpu.CompilerParams(
            collective_id=0, has_side_effects=True, vmem_limit_bytes=60 * 1024 * 1024
        ),
    )(queries, keys, values, jnp.swapaxes(tile_lists, 1, 2), tile_counts)


def solution(mesh):
    placed = (
        P(("grp", "sq"), None),
        P(("grp", "sq"), None),
        P(("grp", "sq"), None),
        P("grp", None, None),
        P("grp", None),
    )
    return jax.shard_map(
        body, mesh=mesh, in_specs=placed, out_specs=P(("grp", "sq"), None), check_vma=False
    )
```

```python
import functools
import heapq

import jax
import jax.numpy as jnp
from jax import lax
from jax.experimental import pallas as pl
from jax.experimental.pallas import tpu as pltpu
from jax.sharding import PartitionSpec as P

MESH = pl.DeviceIdType.MESH
HEAD_DIM = 128
TILE = 128
CHIPS = 8
JOINT = 4
LOW = -1e30
LOG2E = 1.4426950408889634

DO_COMM = True
DO_COMPUTE = True

PIECE, HOP, WORK, BEGIN, AHEAD, FAR = 2.8, 3.0, 3.8, 1.0, 3.0, 1.5


def plain(first, third, fourth):
    route = {0: first, 1: (3, 4), 2: third, 3: fourth}
    return {}, route | {source: (7, None) for source in (4, 5, 6)}


PLAN = (
    plain((3, 4), (4, 5), (7, None)),
    plain((2, 3), (4, 5), (7, None)),
    ({7: 6}, {source: (6, None) for source in range(6)} | {7: (None, 6)}),
    plain((4, 5), (4, 5), (7, None)),
    (
        {6: 5, 7: 0},
        {0: (5, None)}
        | {source: (5, 0) for source in (1, 2, 3, 4)}
        | {5: (None, 0), 6: (0, 5), 7: (0, None)},
    ),
    plain((4, 5), (4, 5), (5, 6)),
    plain((3, 4), (5, 6), (5, 6)),
    plain((4, 5), (6, 7), (5, 6)),
)
AWAY = tuple((h, chip, site) for h, (away, _) in enumerate(PLAN) for chip, site in away.items())


def walk(first, last, step):
    path = [first]
    while path[-1] != last:
        path.append((path[-1] + step) % CHIPS)
    return path


def needed(h, chip):
    away = PLAN[h][0]
    if chip in away:
        return 0
    return 1 + max([chip] + [other for other, site in away.items() if site == chip])


def reckon(ready):
    events, count, waiting, busy, arrive, sends = [], 0, {}, set(), {}, []

    def put(time, what):
        nonlocal count
        heapq.heappush(events, (time, count, what))
        count += 1

    for h, (away, route) in enumerate(PLAN):
        for source, ends in route.items():
            for end, step in zip(ends, (1, -1)):
                if end is not None:
                    put(BEGIN, (("kv", h, source), 1, step, walk(source, end, step), 0))
        for chip, site in away.items():
            step = 1 if (site - chip) % CHIPS == 1 else -1
            put(BEGIN + 5.0, (("q", h, chip), 2, step, [chip, site], 0))
            put(ready.get((h, chip), 1e6), (("o", h, chip), 2, -step, [site, chip], 0))
    while events:
        now, _, what = heapq.heappop(events)
        if len(what) == 2:
            link = what
            busy.discard(link)
        else:
            name, size, step, path, at = what
            if at:
                arrive[name, path[at]] = now
            if at == len(path) - 1:
                continue
            link = (step, path[at])
            rank = name[1] - (3 if name[0] != "kv" else 0) - FAR * (len(path) - 1 - at)
            waiting.setdefault(link, []).append((rank, count, what))
        if waiting.get(link) and link not in busy:
            waiting[link].sort()
            name, size, step, path, at = waiting[link].pop(0)[2]
            busy.add(link)
            sends.append((now, name, step, path[at]))
            put(now + size * PIECE, link)
            put(now + size * PIECE + HOP, (name, size, step, path, at + 1))
    return arrive, sends


def schedule():
    ready = {}
    for _ in range(4):
        arrive, sends = reckon(ready)
        full = [max(t for (n, _), t in arrive.items() if n[:2] == ("kv", h)) for h in range(len(PLAN))]
        steps = [(full[h], h, None, None) for h in range(len(PLAN))]
        for h, chip, site in AWAY:
            steps.append((max(full[h], arrive[("q", h, chip), site]) + WORK, h, chip, site))
        steps.sort(key=lambda step: step[0])
        begin = [[] for _ in range(CHIPS)]
        ready = {}
        for chip in range(CHIPS):
            now = 0.0
            for t, h, away, site in steps:
                takes = chip not in PLAN[h][0] if site is None else chip == site
                now = max(now, full[h] if site is None else arrive[("q", h, away), site])
                begin[chip].append((now, takes))
                now += WORK if takes else 0.0
                if takes and site is not None:
                    ready[h, away] = now + 0.5
    work = []
    for chip in range(CHIPS):
        actions = []
        for (name, at), t in arrive.items():
            if at == chip and name[0] != "o":
                actions.append((t, 0, len(actions), ("take", name, 0)))
        for t, name, step, at in sends:
            if at == chip and name[0] != "o":
                here = arrive.get((name, chip), BEGIN + (5.0 if name[0] == "q" else 0.0))
                actions.append((max(here, t - AHEAD), 1, len(actions), ("send", name, step)))
        for h in range(len(PLAN)):
            if needed(h, chip):
                actions.append((BEGIN + 4.0 * h, 2, len(actions), ("give", ("kv", h, chip), 0)))
        actions.sort()
        ends = [BEGIN + 1.0]
        for t, takes in begin[chip]:
            ends += [t + 0.01, t + WORK / 2 if takes else 0.0]
        parts = []
        for end in ends + [1e9]:
            parts.append([action[3] for action in actions if action[0] < end])
            actions = [action for action in actions if action[0] >= end]
        work.append(parts)
    return [step[1:3] for step in steps], work, max(
        [t + WORK * takes for times in begin for t, takes in times] + [t for (n, _), t in arrive.items() if n[0] == "o"]
    )


def kernel(kv_count, group, tiles, q_hbm, k_hbm, v_hbm, lists_hbm, counts_hbm, out_ref, *scratch):
    kv = scratch[:kv_count]
    q_ref, k_ref, v_ref, lists_ref, counts_ref, q_t = scratch[kv_count : kv_count + 6]
    wide_a, wide_b, scores_a, scores_b, best_a, best_b = scratch[kv_count + 6 : kv_count + 12]
    away_q, away_out = scratch[kv_count + 12 : kv_count + 14]
    load, recv, up_sem, down_sem, twin_sem, away_send, away_recv = scratch[kv_count + 14 :]
    loads = [
        pltpu.make_async_copy(src, dst, load.at[i])
        for i, (src, dst) in enumerate(
            (
                (k_hbm, k_ref),
                (v_hbm, v_ref),
                (q_hbm, q_ref),
                (lists_hbm, lists_ref),
                (counts_hbm, counts_ref),
            )
        )
    ]
    for copy in loads:
        copy.start()
    rank = lax.axis_index("sq")
    z, core = rank // 2, rank % 2
    right = lax.rem(z + 1, CHIPS) * 2 + core
    left = lax.rem(z + CHIPS - 1, CHIPS) * 2 + core
    twin = z * 2 + (1 - core)

    barrier = pltpu.get_barrier_semaphore()
    for other in (left, right, twin):
        pl.semaphore_signal(barrier, inc=1, device_id={"sq": other}, device_id_type=MESH)

    wide_a[...] = jnp.zeros_like(wide_a)
    wide_b[...] = jnp.zeros_like(wide_b)
    loads[0].wait()
    loads[1].wait()
    for h in range(kv_count):
        cols = pl.ds(h * HEAD_DIM, HEAD_DIM)
        for half in range(2):
            rows = pl.ds(half * TILE, TILE)
            kv[h][rank * 2 + half, 0] = k_ref[rows, cols]
            kv[h][rank * 2 + half, 1] = v_ref[rows, cols].T
    pl.semaphore_wait(barrier, 3)

    def piece(h, source, sem, target):
        at = kv[h].at[pl.ds(source * 2, 2)]
        return pltpu.make_async_remote_copy(
            src_ref=at,
            dst_ref=at,
            send_sem=sem,
            recv_sem=recv.at[h, source],
            device_id={"sq": target},
            device_id_type=MESH,
        )

    def along(h, source, step):
        sem = (up_sem if step == 1 else down_sem).at[h, source]
        return piece(h, source * 2 + core, sem, right if step == 1 else left)

    def across(h, source):
        return piece(h, source * 2 + core, twin_sem.at[h, source], twin)

    def beyond(kind, h, chip):
        e = [item[:2] for item in AWAY].index((h, chip))
        site = AWAY[e][2]
        goal = site if kind == "q" else chip
        src = q_t.at[pl.ds(h * group * 2, group * 2)] if kind == "q" else away_out.at[e]
        return pltpu.make_async_remote_copy(
            src_ref=src,
            dst_ref=away_q.at[e] if kind == "q" else away_out.at[e],
            send_sem=away_send.at[e, 0 if kind == "q" else 1],
            recv_sem=away_recv.at[e, 0 if kind == "q" else 1],
            device_id={"sq": goal * 2 + core},
            device_id_type=MESH,
        )

    def act(chip, action):
        what, (kind, h, source), step = action
        if what == "take" and kind == "q":
            beyond("q", h, source).wait_recv()
        elif what == "take":
            along(h, source, 1).wait_recv()
            if source < needed(h, chip):
                across(h, source).start()
        elif what == "give":
            across(h, source).start()
        elif kind == "q":
            beyond("q", h, source).start()
        else:
            along(h, source, step).start()

    def settle(h, chip):
        def one(source, carry):
            piece(h, source * 2 + 1 - core, twin_sem.at[h, source], twin).wait_recv()
            return carry

        lax.fori_loop(0, needed(h, chip), one, 0)

    def sent(chip):
        for part in work[chip]:
            for what, (kind, h, source), step in part:
                if what == "send" and kind == "q":
                    beyond("q", h, source).wait_send()
                elif what == "send":
                    along(h, source, step).wait_send()
        for h in range(kv_count):

            def one(source, carry):
                across(h, source).wait_send()
                return carry

            lax.fori_loop(0, needed(h, chip), one, 0)

    key_at = lax.broadcasted_iota(jnp.int32, (TILE, 2 * TILE), 0)
    query_at = lax.rem(lax.broadcasted_iota(jnp.int32, (TILE, 2 * TILE), 1), TILE)
    causal = key_at <= query_at
    factor = (HEAD_DIM**-0.5) * LOG2E

    def pair(first, second):
        return jnp.concatenate([first, second], axis=1)

    def side(x, half):
        return x[:, half * TILE : (half + 1) * TILE]

    def listed(head, owner, half, j):
        return lists_ref[head, j, owner * 2 + half]

    def live(head, owner, j, x, other):
        return pair(
            *[
                jnp.where(j < counts_ref[head, owner * 2 + half], side(x, half), other)
                for half in range(2)
            ]
        )

    def score(h, i, owner, turned, wide, scores, best_ref):
        head = h * group + i
        for half in range(2):
            at = pl.ds(half * TILE, TILE)
            wide[at, at] = turned[i * 2 + half]
        listed_keys = [
            pair(*[kv[h][listed(head, owner, half, j), 0] for half in range(2)]) for j in range(tiles)
        ]
        all_scores = jnp.dot(
            jnp.concatenate(listed_keys, axis=0), wide[...], preferred_element_type=jnp.float32
        )
        best = jnp.full((8, 2 * TILE), LOW, jnp.float32)
        for j in range(tiles):
            s = all_scores[j * TILE : (j + 1) * TILE]
            if j == 0:
                s = jnp.where(causal, s, LOW)
            scores[j] = s
            top = jnp.max(s.reshape(TILE // 8, 8, 2 * TILE), axis=0)
            best = jnp.maximum(best, live(head, owner, j, top, LOW))
        best_ref[...] = best

    def attend(h, i, owner, scores, best_ref, out):
        head = h * group + i
        best = jnp.max(best_ref[...], axis=0, keepdims=True) * factor
        total = jnp.zeros((8, 2 * TILE), jnp.float32)
        result = [jnp.zeros((HEAD_DIM, TILE), jnp.float32)] * 2
        for first in range(0, tiles, JOINT):
            weights = []
            for j in range(first, first + JOINT):
                w = jnp.exp2(scores[j] * factor - live(head, owner, j, best, 1e30))
                total = total + jnp.sum(w.reshape(TILE // 8, 8, 2 * TILE), axis=0)
                weights.append(w.astype(jnp.bfloat16))
            weights = jnp.concatenate(weights, axis=0)
            for half in range(2):
                turned = [kv[h][listed(head, owner, half, j), 1] for j in range(first, first + JOINT)]
                result[half] = result[half] + jnp.dot(
                    jnp.concatenate(turned, axis=1),
                    side(weights, half),
                    preferred_element_type=jnp.float32,
                )
        scale = 1.0 / jnp.sum(total, axis=0, keepdims=True)
        for half in range(2):
            out[
                pl.ds(half * TILE, TILE),
                pl.ds(pl.multiple_of(i * HEAD_DIM, HEAD_DIM), HEAD_DIM),
            ] = (result[half] * side(scale, half)).T.astype(jnp.bfloat16)

    steps, work, _ = schedule()

    def pass_on(number, settling, when=None):
        if not DO_COMM:
            return
        for chip in range(CHIPS):
            if not work[chip][number] and (settling is None or not needed(settling, chip)):
                continue

            @pl.when(z == chip if when is None else (z == chip) & when)
            def _():
                for action in work[chip][number]:
                    act(chip, action)
                if settling is not None:
                    settle(settling, chip)

    def attend_group(h, owner, turned, out, number):
        score(h, 0, owner, turned, wide_a, scores_a, best_a)

        def step(k, carry):
            i = 2 * k
            pass_on(number, None, k == 1)
            score(h, i + 1, owner, turned, wide_b, scores_b, best_b)
            attend(h, i, owner, scores_a, best_a, out)
            score(h, jnp.minimum(i + 2, group - 1), owner, turned, wide_a, scores_a, best_a)
            attend(h, i + 1, owner, scores_b, best_b, out)
            return carry

        lax.fori_loop(0, group // 2, step, 0)

    def turn(head, carry):
        for half in range(2):
            cols = pl.ds(pl.multiple_of(head * HEAD_DIM, HEAD_DIM), HEAD_DIM)
            q_t[head * 2 + half] = q_ref[pl.ds(half * TILE, TILE), cols].T
        return carry

    pass_on(0, None)
    for copy in loads[2:]:
        copy.wait()
    lax.fori_loop(0, kv_count * group, turn, 0)
    for number, (h, chip) in enumerate(steps):
        pass_on(2 * number + 1, h if chip is None else None)
        columns = pl.ds(h * group * HEAD_DIM, group * HEAD_DIM)
        if chip is None:
            here = z >= 0
            for other in PLAN[h][0]:
                here = here & (z != other)

            @pl.when(here)
            def _():
                if DO_COMPUTE:
                    turned = q_t.at[pl.ds(h * group * 2, group * 2)]
                    attend_group(h, rank, turned, out_ref.at[:, columns], 2 * number + 2)

        else:
            e = [item[:2] for item in AWAY].index((h, chip))

            @pl.when(z == AWAY[e][2])
            def _():
                if DO_COMPUTE:
                    attend_group(h, chip * 2 + core, away_q.at[e], away_out.at[e], 2 * number + 2)
                if DO_COMM:
                    beyond("o", h, chip).start()

    pass_on(2 * len(steps) + 1, None)
    if DO_COMM:
        for e, (h, chip, site) in enumerate(AWAY):

            @pl.when(z == chip)
            def _():
                beyond("o", h, chip).wait_recv()
                out_ref[:, pl.ds(h * group * HEAD_DIM, group * HEAD_DIM)] = away_out[e]

            @pl.when(z == site)
            def _():
                beyond("o", h, chip).wait_send()

        for chip in range(CHIPS):

            @pl.when(z == chip)
            def _():
                sent(chip)


def body(queries, keys, values, tile_lists, tile_counts):
    rows, width = queries.shape
    kv_count = keys.shape[1] // HEAD_DIM
    heads, blocks, tiles = tile_lists.shape
    group = heads // kv_count
    ranks = lax.axis_size("sq")
    hbm = pl.BlockSpec(memory_space=pltpu.HBM)
    scores = pltpu.VMEM((tiles, TILE, 2 * TILE), jnp.float32)
    wide = pltpu.VMEM((2 * TILE, 2 * TILE), jnp.bfloat16)
    best = pltpu.VMEM((8, 2 * TILE), jnp.float32)
    return pl.pallas_call(
        functools.partial(kernel, kv_count, group, tiles),
        out_shape=jax.ShapeDtypeStruct((rows, width), jnp.bfloat16),
        in_specs=[hbm] * 5,
        out_specs=pl.BlockSpec(memory_space=pltpu.VMEM),
        scratch_shapes=[pltpu.VMEM((blocks, 2, TILE, HEAD_DIM), jnp.bfloat16)] * kv_count
        + [
            pltpu.VMEM(queries.shape, jnp.bfloat16),
            pltpu.VMEM(keys.shape, jnp.bfloat16),
            pltpu.VMEM(values.shape, jnp.bfloat16),
            pltpu.SMEM((heads, tiles, blocks), jnp.int32),
            pltpu.SMEM(tile_counts.shape, jnp.int32),
            pltpu.VMEM((heads * 2, HEAD_DIM, TILE), jnp.bfloat16),
            wide,
            wide,
            scores,
            scores,
            best,
            best,
            pltpu.VMEM((len(AWAY), group * 2, HEAD_DIM, TILE), jnp.bfloat16),
            pltpu.VMEM((len(AWAY), rows, group * HEAD_DIM), jnp.bfloat16),
            pltpu.SemaphoreType.DMA((5,)),
            pltpu.SemaphoreType.DMA((kv_count, ranks)),
            pltpu.SemaphoreType.DMA((kv_count, CHIPS)),
            pltpu.SemaphoreType.DMA((kv_count, CHIPS)),
            pltpu.SemaphoreType.DMA((kv_count, CHIPS)),
            pltpu.SemaphoreType.DMA((len(AWAY), 2)),
            pltpu.SemaphoreType.DMA((len(AWAY), 2)),
        ],
        compiler_params=pltpu.CompilerParams(
            collective_id=0, has_side_effects=True, vmem_limit_bytes=34 * 1024 * 1024
        ),
    )(
        *[
            pltpu.with_memory_space_constraint(x, pltpu.HBM)
            for x in (queries, keys, values, jnp.swapaxes(tile_lists, 1, 2), tile_counts)
        ]
    )


def solution(mesh):
    placed = (
        P(("grp", "sq"), None),
        P(("grp", "sq"), None),
        P(("grp", "sq"), None),
        P("grp", None, None),
        P("grp", None),
    )
    return jax.shard_map(
        body, mesh=mesh, in_specs=placed, out_specs=P(("grp", "sq"), None), check_vma=False
    )
```

```python
import functools
import heapq

import jax
import jax.numpy as jnp
from jax import lax
from jax.experimental import pallas as pl
from jax.experimental.pallas import tpu as pltpu
from jax.sharding import PartitionSpec as P

MESH = pl.DeviceIdType.MESH
HEAD_DIM = 128
TILE = 128
CHIPS = 8
JOINT = 2
LOW = -1e30
LOG2E = 1.4426950408889634

DO_COMM = True
DO_COMPUTE = True

PIECE, HOP, WORK, BEGIN, AHEAD, FAR = 2.8, 3.0, 3.8, 1.0, 3.0, 1.5


def plain(first, third, fourth):
    route = {0: first, 1: (3, 4), 2: third, 3: fourth}
    return {}, route | {source: (7, None) for source in (4, 5, 6)}


PLAN = (
    plain((3, 4), (4, 5), (7, None)),
    plain((2, 3), (4, 5), (7, None)),
    ({7: 6}, {source: (6, None) for source in range(6)} | {7: (None, 6)}),
    plain((4, 5), (4, 5), (7, None)),
    (
        {6: 5, 7: 0},
        {0: (5, None)}
        | {source: (5, 0) for source in (1, 2, 3, 4)}
        | {5: (None, 0), 6: (0, 5), 7: (0, None)},
    ),
    plain((4, 5), (4, 5), (5, 6)),
    plain((3, 4), (5, 6), (5, 6)),
    plain((4, 5), (6, 7), (5, 6)),
)
AWAY = tuple((h, chip, site) for h, (away, _) in enumerate(PLAN) for chip, site in away.items())


def walk(first, last, step):
    path = [first]
    while path[-1] != last:
        path.append((path[-1] + step) % CHIPS)
    return path


def needed(h, chip):
    away = PLAN[h][0]
    if chip in away:
        return 0
    return 1 + max([chip] + [other for other, site in away.items() if site == chip])


def reckon(ready):
    events, count, waiting, busy, arrive, sends = [], 0, {}, set(), {}, []

    def put(time, what):
        nonlocal count
        heapq.heappush(events, (time, count, what))
        count += 1

    for h, (away, route) in enumerate(PLAN):
        for source, ends in route.items():
            for end, step in zip(ends, (1, -1)):
                if end is not None:
                    put(BEGIN, (("kv", h, source), 1, step, walk(source, end, step), 0))
        for chip, site in away.items():
            step = 1 if (site - chip) % CHIPS == 1 else -1
            put(BEGIN + 5.0, (("q", h, chip), 2, step, [chip, site], 0))
            put(ready.get((h, chip), 1e6), (("o", h, chip), 2, -step, [site, chip], 0))
    while events:
        now, _, what = heapq.heappop(events)
        if len(what) == 2:
            link = what
            busy.discard(link)
        else:
            name, size, step, path, at = what
            if at:
                arrive[name, path[at]] = now
            if at == len(path) - 1:
                continue
            link = (step, path[at])
            rank = name[1] - (3 if name[0] != "kv" else 0) - FAR * (len(path) - 1 - at)
            waiting.setdefault(link, []).append((rank, count, what))
        if waiting.get(link) and link not in busy:
            waiting[link].sort()
            name, size, step, path, at = waiting[link].pop(0)[2]
            busy.add(link)
            sends.append((now, name, step, path[at]))
            put(now + size * PIECE, link)
            put(now + size * PIECE + HOP, (name, size, step, path, at + 1))
    return arrive, sends


def schedule():
    ready = {}
    for _ in range(4):
        arrive, sends = reckon(ready)
        full = [max(t for (n, _), t in arrive.items() if n[:2] == ("kv", h)) for h in range(len(PLAN))]
        steps = [(full[h], h, None, None) for h in range(len(PLAN))]
        for h, chip, site in AWAY:
            steps.append((max(full[h], arrive[("q", h, chip), site]) + WORK, h, chip, site))
        steps.sort(key=lambda step: step[0])
        begin = [[] for _ in range(CHIPS)]
        ready = {}
        for chip in range(CHIPS):
            now = 0.0
            for t, h, away, site in steps:
                takes = chip not in PLAN[h][0] if site is None else chip == site
                now = max(now, full[h] if site is None else arrive[("q", h, away), site])
                begin[chip].append((now, takes))
                now += WORK if takes else 0.0
                if takes and site is not None:
                    ready[h, away] = now + 0.5
    work = []
    for chip in range(CHIPS):
        actions = []
        for (name, at), t in arrive.items():
            if at == chip and name[0] != "o":
                actions.append((t, 0, len(actions), ("take", name, 0)))
                if name[0] == "kv" and name[2] < needed(name[1], chip):
                    actions.append((t, 2, len(actions), ("give", name, 0)))
        for t, name, step, at in sends:
            if at == chip and name[0] != "o":
                here = arrive.get((name, chip), BEGIN + (5.0 if name[0] == "q" else 0.0))
                actions.append((max(here, t - AHEAD), 1, len(actions), ("send", name, step)))
        for h in range(len(PLAN)):
            if needed(h, chip):
                actions.append((BEGIN + 4.0 * h, 2, len(actions), ("give", ("kv", h, chip), 0)))
        actions.sort()
        ends = [BEGIN + 1.0]
        for t, takes in begin[chip]:
            ends += [t + 0.01, t + WORK / 2 if takes else 0.0]
        parts = []
        for end in ends + [1e9]:
            parts.append([action[3] for action in actions if action[0] < end])
            actions = [action for action in actions if action[0] >= end]
        work.append(parts)
    return [step[1:3] for step in steps], work, max(
        [t + WORK * takes for times in begin for t, takes in times] + [t for (n, _), t in arrive.items() if n[0] == "o"]
    )


def kernel(kv_count, group, tiles, q_hbm, k_hbm, v_hbm, lists_hbm, counts_hbm, out_ref, *scratch):
    kv = scratch[:kv_count]
    q_ref, k_ref, v_ref, lists_ref, counts_ref, q_t = scratch[kv_count : kv_count + 6]
    wide_a, wide_b, scores_a, scores_b, best_a, best_b = scratch[kv_count + 6 : kv_count + 12]
    away_q, away_out = scratch[kv_count + 12 : kv_count + 14]
    load, recv, up_sem, down_sem, twin_sem, away_send, away_recv = scratch[kv_count + 14 :]
    loads = [
        pltpu.make_async_copy(src, dst, load.at[i])
        for i, (src, dst) in enumerate(
            (
                (k_hbm, k_ref),
                (v_hbm, v_ref),
                (q_hbm, q_ref),
                (lists_hbm, lists_ref),
                (counts_hbm, counts_ref),
            )
        )
    ]
    for copy in loads:
        copy.start()
    rank = lax.axis_index("sq")
    z, core = rank // 2, rank % 2
    right = lax.rem(z + 1, CHIPS) * 2 + core
    left = lax.rem(z + CHIPS - 1, CHIPS) * 2 + core
    twin = z * 2 + (1 - core)

    barrier = pltpu.get_barrier_semaphore()
    for other in (left, right, twin):
        pl.semaphore_signal(barrier, inc=1, device_id={"sq": other}, device_id_type=MESH)

    loads[0].wait()
    loads[1].wait()
    for h in range(kv_count):
        cols = pl.ds(h * HEAD_DIM, HEAD_DIM)
        for half in range(2):
            rows = pl.ds(half * TILE, TILE)
            kv[h][rank * 2 + half, 0] = k_ref[rows, cols]
            kv[h][rank * 2 + half, 1] = v_ref[rows, cols].T
    pl.semaphore_wait(barrier, 3)

    def piece(h, source, sem, target):
        at = kv[h].at[pl.ds(source * 2, 2)]
        return pltpu.make_async_remote_copy(
            src_ref=at,
            dst_ref=at,
            send_sem=sem,
            recv_sem=recv.at[h, source],
            device_id={"sq": target},
            device_id_type=MESH,
        )

    def along(h, source, step):
        sem = (up_sem if step == 1 else down_sem).at[h, source]
        return piece(h, source * 2 + core, sem, right if step == 1 else left)

    def across(h, source):
        return piece(h, source * 2 + core, twin_sem.at[h, source], twin)

    def beyond(kind, h, chip):
        e = [item[:2] for item in AWAY].index((h, chip))
        site = AWAY[e][2]
        goal = site if kind == "q" else chip
        src = q_t.at[pl.ds(h * group * 2, group * 2)] if kind == "q" else away_out.at[e]
        return pltpu.make_async_remote_copy(
            src_ref=src,
            dst_ref=away_q.at[e] if kind == "q" else away_out.at[e],
            send_sem=away_send.at[e, 0 if kind == "q" else 1],
            recv_sem=away_recv.at[e, 0 if kind == "q" else 1],
            device_id={"sq": goal * 2 + core},
            device_id_type=MESH,
        )

    def act(chip, action):
        what, (kind, h, source), step = action
        if what == "take" and kind == "q":
            beyond("q", h, source).wait_recv()
        elif what == "take":
            along(h, source, 1).wait_recv()
        elif what == "give":
            across(h, source).start()
        elif kind == "q":
            beyond("q", h, source).start()
        else:
            along(h, source, step).start()

    def settle(h, chip):
        def one(source, carry):
            piece(h, source * 2 + 1 - core, twin_sem.at[h, source], twin).wait_recv()
            return carry

        lax.fori_loop(0, needed(h, chip), one, 0)

    def sent(chip):
        for part in work[chip]:
            for what, (kind, h, source), step in part:
                if what == "send" and kind == "q":
                    beyond("q", h, source).wait_send()
                elif what == "send":
                    along(h, source, step).wait_send()
        for h in range(kv_count):

            def one(source, carry):
                across(h, source).wait_send()
                return carry

            lax.fori_loop(0, needed(h, chip), one, 0)

    key_at = lax.broadcasted_iota(jnp.int32, (TILE, 2 * TILE), 0)
    query_at = lax.rem(lax.broadcasted_iota(jnp.int32, (TILE, 2 * TILE), 1), TILE)
    causal = key_at <= query_at
    factor = (HEAD_DIM**-0.5) * LOG2E

    def pair(first, second):
        return jnp.concatenate([first, second], axis=1)

    def side(x, half):
        return x[:, half * TILE : (half + 1) * TILE]

    def listed(head, owner, half, j):
        return lists_ref[head, j, owner * 2 + half]

    def live(head, owner, j, x, other):
        return pair(
            *[
                jnp.where(j < counts_ref[head, owner * 2 + half], side(x, half), other)
                for half in range(2)
            ]
        )

    def score(h, i, owner, turned, wide, scores, best_ref):
        head = h * group + i
        for half in range(2):
            at = pl.ds(half * TILE, TILE)
            wide[at, at] = turned[i * 2 + half]
        listed_keys = [
            pair(*[kv[h][listed(head, owner, half, j), 0] for half in range(2)]) for j in range(tiles)
        ]
        all_scores = jnp.dot(
            jnp.concatenate(listed_keys, axis=0), wide[...], preferred_element_type=jnp.float32
        )
        best = jnp.full((8, 2 * TILE), LOW, jnp.float32)
        for j in range(tiles):
            s = all_scores[j * TILE : (j + 1) * TILE]
            if j == 0:
                s = jnp.where(causal, s, LOW)
            scores[j] = s
            top = jnp.max(s.reshape(TILE // 8, 8, 2 * TILE), axis=0)
            best = jnp.maximum(best, live(head, owner, j, top, LOW))
        best_ref[...] = best

    def attend(h, i, owner, scores, best_ref, out):
        head = h * group + i
        best = jnp.max(best_ref[...], axis=0, keepdims=True) * factor
        total = jnp.zeros((8, 2 * TILE), jnp.float32)
        result = [jnp.zeros((HEAD_DIM, TILE), jnp.float32)] * 2
        for first in range(0, tiles, JOINT):
            weights = []
            for j in range(first, first + JOINT):
                w = jnp.exp2(scores[j] * factor - live(head, owner, j, best, 1e30))
                total = total + jnp.sum(w.reshape(TILE // 8, 8, 2 * TILE), axis=0)
                weights.append(w.astype(jnp.bfloat16))
            weights = jnp.concatenate(weights, axis=0)
            for half in range(2):
                turned = [kv[h][listed(head, owner, half, j), 1] for j in range(first, first + JOINT)]
                result[half] = result[half] + jnp.dot(
                    jnp.concatenate(turned, axis=1),
                    side(weights, half),
                    preferred_element_type=jnp.float32,
                )
        scale = 1.0 / jnp.sum(total, axis=0, keepdims=True)
        for half in range(2):
            out[
                pl.ds(half * TILE, TILE),
                pl.ds(pl.multiple_of(i * HEAD_DIM, HEAD_DIM), HEAD_DIM),
            ] = (result[half] * side(scale, half)).T.astype(jnp.bfloat16)

    steps, work, _ = schedule()

    def pass_on(number, settling, when=None):
        if not DO_COMM:
            return
        for chip in range(CHIPS):
            if not work[chip][number] and (settling is None or not needed(settling, chip)):
                continue

            @pl.when(z == chip if when is None else (z == chip) & when)
            def _():
                for action in work[chip][number]:
                    act(chip, action)
                if settling is not None:
                    settle(settling, chip)

    def attend_group(h, owner, turned, out, number):
        score(h, 0, owner, turned, wide_a, scores_a, best_a)

        def step(k, carry):
            i = 2 * k
            pass_on(number, None, k == 1)
            score(h, i + 1, owner, turned, wide_b, scores_b, best_b)
            attend(h, i, owner, scores_a, best_a, out)
            score(h, jnp.minimum(i + 2, group - 1), owner, turned, wide_a, scores_a, best_a)
            attend(h, i + 1, owner, scores_b, best_b, out)
            return carry

        lax.fori_loop(0, group // 2, step, 0)

    def turn(head, carry):
        for half in range(2):
            cols = pl.ds(pl.multiple_of(head * HEAD_DIM, HEAD_DIM), HEAD_DIM)
            q_t[head * 2 + half] = q_ref[pl.ds(half * TILE, TILE), cols].T
        return carry

    pass_on(0, None)
    wide_a[...] = jnp.zeros_like(wide_a)
    wide_b[...] = jnp.zeros_like(wide_b)
    for copy in loads[2:]:
        copy.wait()
    lax.fori_loop(0, kv_count * group, turn, 0)
    for number, (h, chip) in enumerate(steps):
        pass_on(2 * number + 1, h if chip is None else None)
        columns = pl.ds(h * group * HEAD_DIM, group * HEAD_DIM)
        if chip is None:
            here = z >= 0
            for other in PLAN[h][0]:
                here = here & (z != other)

            @pl.when(here)
            def _():
                if not DO_COMPUTE:
                    pass_on(2 * number + 2, None)
                if DO_COMPUTE:
                    turned = q_t.at[pl.ds(h * group * 2, group * 2)]
                    attend_group(h, rank, turned, out_ref.at[:, columns], 2 * number + 2)

        else:
            e = [item[:2] for item in AWAY].index((h, chip))

            @pl.when(z == AWAY[e][2])
            def _():
                if not DO_COMPUTE:
                    pass_on(2 * number + 2, None)
                if DO_COMPUTE:
                    attend_group(h, chip * 2 + core, away_q.at[e], away_out.at[e], 2 * number + 2)
                if DO_COMM:
                    beyond("o", h, chip).start()

    pass_on(2 * len(steps) + 1, None)
    if DO_COMM:
        for e, (h, chip, site) in enumerate(AWAY):

            @pl.when(z == chip)
            def _():
                beyond("o", h, chip).wait_recv()
                out_ref[:, pl.ds(h * group * HEAD_DIM, group * HEAD_DIM)] = away_out[e]

            @pl.when(z == site)
            def _():
                beyond("o", h, chip).wait_send()

        for chip in range(CHIPS):

            @pl.when(z == chip)
            def _():
                sent(chip)


def body(queries, keys, values, tile_lists, tile_counts):
    rows, width = queries.shape
    kv_count = keys.shape[1] // HEAD_DIM
    heads, blocks, tiles = tile_lists.shape
    group = heads // kv_count
    ranks = lax.axis_size("sq")
    hbm = pl.BlockSpec(memory_space=pltpu.HBM)
    scores = pltpu.VMEM((tiles, TILE, 2 * TILE), jnp.float32)
    wide = pltpu.VMEM((2 * TILE, 2 * TILE), jnp.bfloat16)
    best = pltpu.VMEM((8, 2 * TILE), jnp.float32)
    return pl.pallas_call(
        functools.partial(kernel, kv_count, group, tiles),
        out_shape=jax.ShapeDtypeStruct((rows, width), jnp.bfloat16),
        in_specs=[hbm] * 5,
        out_specs=pl.BlockSpec(memory_space=pltpu.VMEM),
        scratch_shapes=[pltpu.VMEM((blocks, 2, TILE, HEAD_DIM), jnp.bfloat16)] * kv_count
        + [
            pltpu.VMEM(queries.shape, jnp.bfloat16),
            pltpu.VMEM(keys.shape, jnp.bfloat16),
            pltpu.VMEM(values.shape, jnp.bfloat16),
            pltpu.SMEM((heads, tiles, blocks), jnp.int32),
            pltpu.SMEM(tile_counts.shape, jnp.int32),
            pltpu.VMEM((heads * 2, HEAD_DIM, TILE), jnp.bfloat16),
            wide,
            wide,
            scores,
            scores,
            best,
            best,
            pltpu.VMEM((len(AWAY), group * 2, HEAD_DIM, TILE), jnp.bfloat16),
            pltpu.VMEM((len(AWAY), rows, group * HEAD_DIM), jnp.bfloat16),
            pltpu.SemaphoreType.DMA((5,)),
            pltpu.SemaphoreType.DMA((kv_count, ranks)),
            pltpu.SemaphoreType.DMA((kv_count, CHIPS)),
            pltpu.SemaphoreType.DMA((kv_count, CHIPS)),
            pltpu.SemaphoreType.DMA((kv_count, CHIPS)),
            pltpu.SemaphoreType.DMA((len(AWAY), 2)),
            pltpu.SemaphoreType.DMA((len(AWAY), 2)),
        ],
        compiler_params=pltpu.CompilerParams(
            collective_id=0, has_side_effects=True, vmem_limit_bytes=34 * 1024 * 1024
        ),
    )(
        *[
            pltpu.with_memory_space_constraint(x, pltpu.HBM)
            for x in (queries, keys, values, jnp.swapaxes(tile_lists, 1, 2), tile_counts)
        ]
    )


def solution(mesh):
    placed = (
        P(("grp", "sq"), None),
        P(("grp", "sq"), None),
        P(("grp", "sq"), None),
        P("grp", None, None),
        P("grp", None),
    )
    return jax.shard_map(
        body, mesh=mesh, in_specs=placed, out_specs=P(("grp", "sq"), None), check_vma=False
    )
```
